32 devices in a mesh: fsdp: 16 (over z, x, core), tp: 2 (over y).
Axes of the slice: x: 2, y: 2, z: 4, core: 2. Of those that a mesh axis runs over, the one named last changes fastest.
Arguments:
- activations: bfloat16 [4096, 8192], P('fsdp'), may hold values from -6 to 6
- grad_output: bfloat16 [4096, 28672], P('fsdp', 'tp'), may hold values from -0.25 to 0.25
- projector: bfloat16 [8192, 1024], P('fsdp'), may hold values from -0.09375 to 0.09375
- first_moment: float32 [1024, 28672], P('fsdp', 'tp'), may hold values from -0.625 to 0.625
- second_moment: float32 [1024, 28672], P('fsdp', 'tp'), may hold values from 0.01 to 0.5
Outputs:
- new_first: float32 [1024, 28672], P('fsdp', 'tp')
- new_second: float32 [1024, 28672], P('fsdp', 'tp')
- weight_update: bfloat16 [8192, 28672], P('fsdp', 'tp')
The draws below stay inside these ranges and needn't reach their ends.
All inputs are finite; a program needn't handle non-finite values.
Results may differ from the reference program's by a relative error of at most 0.0059.
Values may be sent and summed in bfloat16 or wider, within the bound.
A program may use at most 192 MiB of HBM per device.

```python
import math
import jax
import jax.numpy as jnp

D = 8192
FF = 28672
R = 1024
TOKENS = 4096


def raised(array, rng, source, target, shards_of, factor):
    owner, partner = [(jnp.arange(array.shape[position]) // (array.shape[position] // shards_of)).reshape([-1 if axis == position else 1 for axis in range(array.ndim)]) for position in (source, target)]
    chosen = jax.random.permutation(rng, shards_of)[partner]
    strong = (owner == chosen) | (owner == (partner + shards_of // 2) % shards_of)
    return jnp.where(strong, factor * array, array)


def shard_levels(own_key, extent, shards, smallest, top_value):
    def one(position, parts):
        steps = jax.random.uniform(jax.random.fold_in(jax.random.fold_in(own_key, 6), position), (parts,), jnp.float32, smallest / len(shards), top_value / len(shards))
        return jnp.repeat(jnp.exp(steps), extent[position] // parts).reshape((-1,) + (1,) * (len(extent) - position - 1))

    factor_of = one(*shards[0])
    for cut in shards[1:]:
        factor_of = factor_of * one(*cut)
    return factor_of


def noise(rng, shape, spread, reach, split=(), kind=jnp.bfloat16):
    factor_of = shard_levels(rng, shape, split, -0.22, 0.18) if split else 1.0
    result = jax.random.normal(rng, shape, jnp.float32) * spread * factor_of
    return jnp.minimum(jnp.maximum(result, -reach), reach).astype(kind)


def heavy_noise(key, extent, spread, limit, split, heavy, dtype=jnp.bfloat16):
    values = spread * jax.random.normal(key, extent, jnp.float32)
    if split:
        values = values * shard_levels(key, extent, split, -0.22, 0.18)
    return jnp.clip(raised(values, jax.random.fold_in(key, 3), *heavy), -limit, limit).astype(dtype)


def setup_inputs(seed: int = 0) -> dict:
    keys = jax.random.split(jax.random.key(seed), 6)
    activations = noise(keys[0], (TOKENS, D), 1.0, 6.0, ((0, 16),))
    grad_output = noise(keys[1], (TOKENS, FF), (3 * TOKENS ** -0.5), 0.25, ((0, 16), (1, 2)))
    projector = heavy_noise(keys[2], (D, R), D ** -0.5, 0.09375, ((0, 16),), (0, 1, 16, 2.0))
    first_moment = noise(keys[3], (R, FF), 0.1, 0.625, ((0, 16), (1, 2)), jnp.float32)
    second_moment = jnp.clip(jnp.exp(math.log(0.5) - 3.912023 * jax.random.uniform(keys[4], (R, FF), jnp.float32) ** shard_levels(keys[4], (R, FF), ((0, 16), (1, 2)), -0.2, 0.2)), 0.01, 0.5)
    return {"activations": activations, "grad_output": grad_output, "projector": projector, "first_moment": first_moment, "second_moment": second_moment}


first_fix = 0.9999734386011124
second_fix = 0.6339676587267705

def reference(activations, grad_output, projector, first_moment, second_moment):
    coords = jnp.dot(activations, projector, preferred_element_type=jnp.float32).astype(jnp.bfloat16)
    lowrank = jnp.dot(coords.T, grad_output, preferred_element_type=jnp.float32)
    new_first = 0.9 * first_moment + 0.1 * lowrank
    new_second = 0.99 * second_moment + 0.01 * lowrank * lowrank
    direction = (new_first / first_fix / (jnp.sqrt(new_second / second_fix) + 1e-08)).astype(jnp.bfloat16)
    weight_update = jnp.dot(projector, direction, preferred_element_type=jnp.float32).astype(jnp.bfloat16)
    return (new_first, new_second, weight_update)
```

```python
import functools

import jax
import jax.numpy as jnp
from jax import lax
from jax.experimental import pallas as pl
from jax.experimental.pallas import tpu as pltpu
from jax.sharding import PartitionSpec as P

first_fix = 0.9999734386011124
second_fix = 0.6339676587267705

MESH = pl.DeviceIdType.MESH
LINE = 4
CORES = 2
CHUNKS = 14
AHEAD = 4
LAG = 4


def reduce_kernel(
    coords_ref, grad_ref, first_ref, second_ref,
    new_first_ref, new_second_ref, direction_ref,
    coords_all, grads, partial, landed,
    coords_send, coords_recv, own_sem, grad_send, grad_recv, part_send, part_recv,
):
    plane = coords_all.shape[0]
    rows = first_ref.shape[0]
    half = first_ref.shape[1] // CORES
    width = half // CHUNKS
    me = lax.axis_index("fsdp")
    tp = lax.axis_index("tp")
    z = lax.div(me, plane)
    slot = lax.rem(me, plane)
    chip = lax.div(slot, CORES)
    core = lax.rem(slot, CORES)

    def in_plane(step):
        return lax.rem(slot + step, plane)

    def on_line(dz, dc):
        return lax.rem(z + dz, LINE), lax.rem(core + dc, CORES)

    line_peers = [(dz, dc) for dz in range(LINE) for dc in range(CORES) if dz or dc]

    def device(z_to, slot_to):
        return (z_to * plane + slot_to, tp)

    barrier = pltpu.get_barrier_semaphore()
    for step in range(1, plane):
        pl.semaphore_signal(barrier, inc=1, device_id=device(z, in_plane(step)), device_id_type=MESH)
    for dz, dc in line_peers:
        if dz:
            z_to, core_to = on_line(dz, dc)
            pl.semaphore_signal(
                barrier, inc=1, device_id=device(z_to, chip * CORES + core_to), device_id_type=MESH
            )
    pl.semaphore_wait(barrier, plane - 1 + (LINE - 1) * CORES)

    def coords_copy(step):
        to = in_plane(step)
        return pltpu.make_async_remote_copy(
            src_ref=coords_ref.at[lax.div(to, CORES)],
            dst_ref=coords_all.at[slot],
            send_sem=coords_send.at[step - 1],
            recv_sem=coords_recv.at[slot],
            device_id=device(z, to),
            device_id_type=MESH,
        )

    def grad_copy(step, i):
        to = in_plane(step)
        start = pl.multiple_of(lax.rem(to, CORES) * half + i * width, 128)
        return pltpu.make_async_remote_copy(
            src_ref=grad_ref.at[:, pl.ds(start, width)],
            dst_ref=grads.at[slot, i],
            send_sem=grad_send.at[step - 1, i],
            recv_sem=grad_recv.at[slot, i],
            device_id=device(z, to),
            device_id_type=MESH,
        )

    def own_copy(i):
        start = pl.multiple_of(core * half + i * width, 128)
        return pltpu.make_async_copy(
            grad_ref.at[:, pl.ds(start, width)], grads.at[slot, i], own_sem.at[i]
        )

    def part_copy(index, i):
        z_to, core_to = on_line(*line_peers[index])
        return pltpu.make_async_remote_copy(
            src_ref=partial.at[z_to * CORES + core_to, i],
            dst_ref=landed.at[core, z, i],
            send_sem=part_send.at[index, i],
            recv_sem=part_recv.at[core, z, i],
            device_id=device(z_to, chip * CORES + core_to),
            device_id_type=MESH,
        )

    def arrived(ref, sem):
        pltpu.make_async_copy(ref, ref, sem).wait()

    def send_grads(i):
        own_copy(i).start()
        for step in range(1, plane):
            grad_copy(step, i).start()

    for step in range(1, plane):
        coords_copy(step).start()
    for i in range(AHEAD):
        send_grads(i)
    coords_all[slot] = coords_ref[chip]
    for step in range(1, plane):
        source = in_plane(step)
        arrived(coords_all.at[source], coords_recv.at[source])

    def multiply(i):
        own_copy(i).wait()
        for step in range(1, plane):
            source = in_plane(step)
            arrived(grads.at[source, i], grad_recv.at[source, i])
        total = jnp.dot(coords_all[0], grads[0, i], preferred_element_type=jnp.float32)
        for source in range(1, plane):
            total += jnp.dot(
                coords_all[source], grads[source, i], preferred_element_type=jnp.float32
            )
        total = total.astype(jnp.bfloat16)
        for block in range(LINE * CORES):
            partial[block, i] = total[block * rows : (block + 1) * rows]
        for index in range(len(line_peers)):
            part_copy(index, i).start()
        landed[core, z, i] = partial[z * CORES + core, i]

    def adam(i):
        for dz, dc in line_peers:
            z_from, core_from = on_line(dz, dc)
            arrived(landed.at[core_from, z_from, i], part_recv.at[core_from, z_from, i])
        for side in range(CORES):
            lowrank = landed[side, 0, i].astype(jnp.float32)
            for z_from in range(1, LINE):
                lowrank += landed[side, z_from, i].astype(jnp.float32)
            columns = pl.ds(pl.multiple_of(side * half + i * width, 128), width)
            new_first = 0.9 * first_ref[:, columns] + 0.1 * lowrank
            new_second = 0.99 * second_ref[:, columns] + 0.01 * lowrank * lowrank
            new_first_ref[:, columns] = new_first
            new_second_ref[:, columns] = new_second
            direction_ref[:, columns] = (
                new_first / first_fix / (jnp.sqrt(new_second / second_fix) + 1e-08)
            ).astype(jnp.bfloat16)

    @pl.loop(0, CHUNKS)
    def _(i):
        @pl.when(i + AHEAD < CHUNKS)
        def _():
            send_grads(i + AHEAD)

        multiply(i)

        @pl.when(i >= LAG)
        def _():
            adam(i - LAG)

    @pl.loop(CHUNKS - LAG, CHUNKS)
    def _(i):
        adam(i)

    for step in range(1, plane):
        coords_copy(step).wait_send()

    @pl.loop(0, CHUNKS)
    def _(i):
        for step in range(1, plane):
            grad_copy(step, i).wait_send()
        for index in range(len(line_peers)):
            part_copy(index, i).wait_send()


def reduced(coords, grad_output, first_moment, second_moment):
    chips, share, tokens = coords.shape
    plane = chips * CORES
    rows, columns = first_moment.shape
    width = columns // CORES // CHUNKS
    peers = LINE * CORES - 1
    vmem = pl.BlockSpec(memory_space=pltpu.VMEM)
    return pl.pallas_call(
        reduce_kernel,
        out_shape=(
            jax.ShapeDtypeStruct((rows, columns), jnp.float32),
            jax.ShapeDtypeStruct((rows, columns), jnp.float32),
            jax.ShapeDtypeStruct((rows, columns), jnp.bfloat16),
        ),
        in_specs=[vmem, pl.BlockSpec(memory_space=pl.ANY), vmem, vmem],
        out_specs=(vmem, vmem, vmem),
        scratch_shapes=[
            pltpu.VMEM((plane, share, tokens), jnp.bfloat16),
            pltpu.VMEM((plane, CHUNKS, tokens, width), jnp.bfloat16),
            pltpu.VMEM((LINE * CORES, CHUNKS, rows, width), jnp.bfloat16),
            pltpu.VMEM((CORES, LINE, CHUNKS, rows, width), jnp.bfloat16),
            pltpu.SemaphoreType.DMA((plane - 1,)),
            pltpu.SemaphoreType.DMA((plane,)),
            pltpu.SemaphoreType.DMA((CHUNKS,)),
            pltpu.SemaphoreType.DMA((plane - 1, CHUNKS)),
            pltpu.SemaphoreType.DMA((plane, CHUNKS)),
            pltpu.SemaphoreType.DMA((peers, CHUNKS)),
            pltpu.SemaphoreType.DMA((CORES, LINE, CHUNKS)),
        ],
        compiler_params=pltpu.CompilerParams(
            collective_id=0, has_side_effects=True, vmem_limit_bytes=58 * 2**20
        ),
        name="reduce_and_step",
    )(coords, grad_output, first_moment, second_moment)


def update_kernel(projector_ref, direction_ref, out_ref):
    out_ref[...] = jnp.dot(
        projector_ref[...], direction_ref[...], preferred_element_type=jnp.float32
    ).astype(jnp.bfloat16)


def back_projected(projector, direction):
    rows, rank = projector.shape
    columns = direction.shape[1]
    width = columns // CHUNKS
    return pl.pallas_call(
        update_kernel,
        out_shape=jax.ShapeDtypeStruct((rows, columns), jnp.bfloat16),
        grid=(CHUNKS,),
        in_specs=[
            pl.BlockSpec((rows, rank), lambda i: (0, 0)),
            pl.BlockSpec((rank, width), lambda i: (0, i)),
        ],
        out_specs=pl.BlockSpec((rows, width), lambda i: (0, i)),
        compiler_params=pltpu.CompilerParams(vmem_limit_bytes=40 * 2**20),
        name="back_project",
    )(projector, direction)


def body(activations, grad_output, projector, first_moment, second_moment):
    rank_width = projector.shape[1]
    tp_count = lax.axis_size("tp")
    tp_place = lax.axis_index("tp")
    chips = lax.axis_size("fsdp") // (LINE * CORES)
    column_count = rank_width // tp_count
    proj_block = lax.dynamic_slice_in_dim(projector, tp_place * column_count, column_count, 1)
    proj_all = lax.all_gather(proj_block, "fsdp", axis=0, tiled=True)
    coords_block = lax.dot_general(
        proj_all, activations, (((0,), (1,)), ((), ())), preferred_element_type=jnp.float32
    ).astype(jnp.bfloat16)
    coords = lax.all_gather(coords_block, "tp", axis=0, tiled=True)
    tokens = coords.shape[1]
    coords = coords.reshape(LINE, chips, -1, tokens).transpose(1, 0, 2, 3)
    coords = coords.reshape(chips, rank_width // chips, tokens)
    new_first, new_second, direction = reduced(coords, grad_output, first_moment, second_moment)
    direction_all = lax.all_gather(direction, "fsdp", axis=0, tiled=True)
    return (new_first, new_second, back_projected(projector, direction_all))


def solution(mesh):
    return jax.shard_map(
        body,
        mesh=mesh,
        in_specs=(
            P("fsdp", None),
            P("fsdp", "tp"),
            P("fsdp", None),
            P("fsdp", "tp"),
            P("fsdp", "tp"),
        ),
        out_specs=(P("fsdp", "tp"), P("fsdp", "tp"), P("fsdp", "tp")),
        check_vma=False,
    )
```

```python
import functools

import jax
import jax.numpy as jnp
from jax import lax
from jax.experimental import pallas as pl
from jax.experimental.pallas import tpu as pltpu
from jax.sharding import PartitionSpec as P

first_fix = 0.9999734386011124
second_fix = 0.6339676587267705

MESH = pl.DeviceIdType.MESH
LINE = 4
CORES = 2
CHUNKS = 14
AHEAD = 4
LAG = 4


def reduce_kernel(
    act_ref, proj_ref, grad_ref, first_ref, second_ref,
    new_first_ref, new_second_ref, direction_ref,
    proj_all, acts, acc, acc_in, coords, coords_all, grads, partial, landed,
    line_send, line_recv, row_send, row_recv, act_sem, act_send, act_recv, acc_send, acc_recv,
    coords_send, coords_recv, own_sem, grad_send, grad_recv, part_send, part_recv,
):
    plane = grads.shape[0]
    chips = plane // CORES
    tps = lax.axis_size("tp")
    parts = coords.shape[0]
    depth = proj_ref.shape[0]
    rows = first_ref.shape[0]
    half = first_ref.shape[1] // CORES
    width = half // CHUNKS
    me = lax.axis_index("fsdp")
    tp = lax.axis_index("tp")
    z = lax.div(me, plane)
    slot = lax.rem(me, plane)
    chip = lax.div(slot, CORES)
    core = lax.rem(slot, CORES)
    sibling = chip * CORES + 1 - core

    def in_plane(step):
        return lax.rem(slot + step, plane)

    def on_line(dz, dc):
        return lax.rem(z + dz, LINE), lax.rem(core + dc, CORES)

    line_peers = [(dz, dc) for dz in range(LINE) for dc in range(CORES) if dz or dc]

    def device(z_to, slot_to, dt=0):
        return (z_to * plane + slot_to, lax.rem(tp + dt, tps) if dt else tp)

    barrier = pltpu.get_barrier_semaphore()
    for step in range(plane):
        for dt in range(tps):
            if step or dt:
                pl.semaphore_signal(
                    barrier, inc=1, device_id=device(z, in_plane(step), dt), device_id_type=MESH
                )
    for dz, dc in line_peers:
        if dz:
            z_to, core_to = on_line(dz, dc)
            pl.semaphore_signal(
                barrier, inc=1, device_id=device(z_to, chip * CORES + core_to), device_id_type=MESH
            )
    pl.semaphore_wait(barrier, plane * tps - 1 + (LINE - 1) * CORES)

    def arrived(ref, sem):
        pltpu.make_async_copy(ref, ref, sem).wait()

    def line_copy(dz):
        z_to, _ = on_line(dz, 0)
        return pltpu.make_async_remote_copy(
            src_ref=proj_ref,
            dst_ref=proj_all.at[z * chips + chip],
            send_sem=line_send.at[dz],
            recv_sem=line_recv.at[z],
            device_id=device(z_to, slot),
            device_id_type=MESH,
        )

    def row_copy(dz, dx):
        z_from, _ = on_line(dz, 0)
        block = z_from * chips + chip
        return pltpu.make_async_remote_copy(
            src_ref=proj_all.at[block] if dz else proj_ref,
            dst_ref=proj_all.at[block],
            send_sem=row_send.at[dx, dz],
            recv_sem=row_recv.at[block],
            device_id=device(z, lax.rem(chip + dx, chips) * CORES + core),
            device_id_type=MESH,
        )

    def act_columns(block, side):
        return act_ref.at[:, pl.ds(pl.multiple_of((block * CORES + side) * depth, 128), depth)]

    def act_own(block):
        return pltpu.make_async_copy(act_columns(block, core), acts.at[block, 0], act_sem.at[block])

    def act_copy(block):
        return pltpu.make_async_remote_copy(
            src_ref=act_columns(block, 1 - core),
            dst_ref=acts.at[block, 1],
            send_sem=act_send.at[block],
            recv_sem=act_recv.at[block],
            device_id=device(z, sibling),
            device_id_type=MESH,
        )

    def acc_copy():
        return pltpu.make_async_remote_copy(
            src_ref=acc.at[1],
            dst_ref=acc_in,
            send_sem=acc_send,
            recv_sem=acc_recv,
            device_id=device(z, sibling),
            device_id_type=MESH,
        )

    def coords_place(q):
        place = tp * parts + q
        return lax.rem(place, chips), lax.div(place, chips)

    def coords_copy(q, dc, dt):
        chip_to, block = coords_place(q)
        return pltpu.make_async_remote_copy(
            src_ref=coords.at[q],
            dst_ref=coords_all.at[slot, block],
            send_sem=coords_send.at[q, dc * tps + dt],
            recv_sem=coords_recv.at[slot, block],
            device_id=device(z, chip_to * CORES + lax.rem(core + dc, CORES), dt),
            device_id_type=MESH,
        )

    def each_coords_copy(act):
        for q in range(parts):
            chip_to, _ = coords_place(q)
            for dc in range(CORES):
                for dt in range(tps):
                    if dc or dt:
                        act(coords_copy(q, dc, dt))
                    else:
                        @pl.when(chip_to != chip)
                        def _():
                            act(coords_copy(q, 0, 0))

    def grad_copy(step, i):
        to = in_plane(step)
        start = pl.multiple_of(lax.rem(to, CORES) * half + i * width, 128)
        return pltpu.make_async_remote_copy(
            src_ref=grad_ref.at[:, pl.ds(start, width)],
            dst_ref=grads.at[slot, i],
            send_sem=grad_send.at[step - 1, i],
            recv_sem=grad_recv.at[slot, i],
            device_id=device(z, to),
            device_id_type=MESH,
        )

    def own_copy(i):
        start = pl.multiple_of(core * half + i * width, 128)
        return pltpu.make_async_copy(
            grad_ref.at[:, pl.ds(start, width)], grads.at[slot, i], own_sem.at[i]
        )

    def part_copy(index, i):
        z_to, core_to = on_line(*line_peers[index])
        return pltpu.make_async_remote_copy(
            src_ref=partial.at[z_to * CORES + core_to, i],
            dst_ref=landed.at[core, z, i],
            send_sem=part_send.at[index, i],
            recv_sem=part_recv.at[core, z, i],
            device_id=device(z_to, chip * CORES + core_to),
            device_id_type=MESH,
        )

    def send_grads(i):
        own_copy(i).start()
        for step in range(1, plane):
            grad_copy(step, i).start()

    blocks = acts.shape[0]
    for dz in range(1, LINE):
        line_copy(dz).start()
    for dx in range(1, chips):
        row_copy(0, dx).start()
    for block in range(blocks):
        act_own(block).start()
        act_copy(block).start()
    send_grads(0)
    acc[...] = jnp.zeros_like(acc)

    def accumulate(block, features):
        act_own(block).wait()
        arrived(acts.at[block, 1], act_recv.at[block])
        tokens = acts.shape[2]
        both = acts[block].reshape(CORES * tokens, depth)
        acc[...] += jnp.dot(both, features, preferred_element_type=jnp.float32).reshape(acc.shape)

    for dz in range(LINE):
        z_from, _ = on_line(dz, 0)
        block = z_from * chips + chip
        if dz:
            arrived(proj_all.at[block], line_recv.at[z_from])
            for dx in range(1, chips):
                row_copy(dz, dx).start()
            if dz < AHEAD:
                send_grads(dz)
            accumulate(block, proj_all[block])
        else:
            accumulate(block, proj_ref[...])
    for dz in range(LINE):
        z_from, _ = on_line(dz, 0)
        for dx in range(1, chips):
            block = z_from * chips + lax.rem(chip + dx, chips)
            arrived(proj_all.at[block], row_recv.at[block])
            accumulate(block, proj_all[block])
    acc_copy().start()
    arrived(acc_in, acc_recv)
    summed = jnp.transpose(acc[0] + acc_in[...]).astype(jnp.bfloat16)
    coords[...] = summed.reshape(coords.shape)
    each_coords_copy(lambda copy: copy.start())
    for q in range(parts):
        chip_to, own_block = coords_place(q)

        @pl.when(chip_to == chip)
        def _():
            coords_all[slot, own_block] = coords[q]

    for step in range(plane):
        source = in_plane(step)
        for block in range(LINE):
            if step:
                arrived(coords_all.at[source, block], coords_recv.at[source, block])
            else:
                @pl.when(lax.div(block * chips + chip, parts) != tp)
                def _():
                    arrived(coords_all.at[source, block], coords_recv.at[source, block])

    def multiply(i):
        own_copy(i).wait()
        for step in range(1, plane):
            source = in_plane(step)
            arrived(grads.at[source, i], grad_recv.at[source, i])
        total = 0.0
        for source in range(plane):
            ranks = coords_all[source].reshape(LINE * CORES * rows, -1)
            total += jnp.dot(ranks, grads[source, i], preferred_element_type=jnp.float32)
        total = total.astype(jnp.bfloat16)
        for block in range(LINE * CORES):
            partial[block, i] = total[block * rows : (block + 1) * rows]
        for index in range(len(line_peers)):
            part_copy(index, i).start()
        landed[core, z, i] = partial[z * CORES + core, i]

    def adam(i):
        for dz, dc in line_peers:
            z_from, core_from = on_line(dz, dc)
            arrived(landed.at[core_from, z_from, i], part_recv.at[core_from, z_from, i])
        for side in range(CORES):
            lowrank = landed[side, 0, i].astype(jnp.float32)
            for z_from in range(1, LINE):
                lowrank += landed[side, z_from, i].astype(jnp.float32)
            columns = pl.ds(pl.multiple_of(side * half + i * width, 128), width)
            new_first = 0.9 * first_ref[:, columns] + 0.1 * lowrank
            new_second = 0.99 * second_ref[:, columns] + 0.01 * lowrank * lowrank
            new_first_ref[:, columns] = new_first
            new_second_ref[:, columns] = new_second
            direction_ref[:, columns] = (
                new_first / first_fix / (jnp.sqrt(new_second / second_fix) + 1e-08)
            ).astype(jnp.bfloat16)

    @pl.loop(0, CHUNKS)
    def _(i):
        @pl.when(i + AHEAD < CHUNKS)
        def _():
            send_grads(i + AHEAD)

        multiply(i)

        @pl.when(i >= LAG)
        def _():
            adam(i - LAG)

    @pl.loop(CHUNKS - LAG, CHUNKS)
    def _(i):
        adam(i)

    for dz in range(1, LINE):
        line_copy(dz).wait_send()
    for dz in range(LINE):
        for dx in range(1, chips):
            row_copy(dz, dx).wait_send()
    for block in range(blocks):
        act_copy(block).wait_send()
    acc_copy().wait_send()
    each_coords_copy(lambda copy: copy.wait_send())

    @pl.loop(0, CHUNKS)
    def _(i):
        for step in range(1, plane):
            grad_copy(step, i).wait_send()
        for index in range(len(line_peers)):
            part_copy(index, i).wait_send()


def reduced(activations, proj_block, grad_output, first_moment, second_moment):
    tps = lax.axis_size("tp")
    plane = lax.axis_size("fsdp") // LINE
    blocks = plane * LINE // CORES
    tokens = activations.shape[0]
    depth, ranks = proj_block.shape
    rows, columns = first_moment.shape
    parts = ranks // (CORES * rows)
    width = columns // CORES // CHUNKS
    peers = LINE * CORES - 1
    dma = pltpu.SemaphoreType.DMA
    vmem = pl.BlockSpec(memory_space=pltpu.VMEM)
    hbm = pl.BlockSpec(memory_space=pl.ANY)
    return pl.pallas_call(
        reduce_kernel,
        out_shape=(
            jax.ShapeDtypeStruct((rows, columns), jnp.float32),
            jax.ShapeDtypeStruct((rows, columns), jnp.float32),
            jax.ShapeDtypeStruct((rows, columns), jnp.bfloat16),
        ),
        in_specs=[hbm, vmem, hbm, vmem, vmem],
        out_specs=(vmem, vmem, vmem),
        scratch_shapes=[
            pltpu.VMEM((blocks, depth, ranks), jnp.bfloat16),
            pltpu.VMEM((blocks, CORES, tokens, depth), jnp.bfloat16),
            pltpu.VMEM((CORES, tokens, ranks), jnp.float32),
            pltpu.VMEM((tokens, ranks), jnp.float32),
            pltpu.VMEM((parts, CORES * rows, tokens), jnp.bfloat16),
            pltpu.VMEM((plane, LINE, CORES * rows, tokens), jnp.bfloat16),
            pltpu.VMEM((plane, CHUNKS, tokens, width), jnp.bfloat16),
            pltpu.VMEM((LINE * CORES, CHUNKS, rows, width), jnp.bfloat16),
            pltpu.VMEM((CORES, LINE, CHUNKS, rows, width), jnp.bfloat16),
            dma((LINE,)),
            dma((LINE,)),
            dma((plane // CORES, LINE)),
            dma((blocks,)),
            dma((blocks,)),
            dma((blocks,)),
            dma((blocks,)),
            dma,
            dma,
            dma((parts, CORES * tps)),
            dma((plane, LINE)),
            dma((CHUNKS,)),
            dma((plane - 1, CHUNKS)),
            dma((plane, CHUNKS)),
            dma((peers, CHUNKS)),
            dma((CORES, LINE, CHUNKS)),
        ],
        compiler_params=pltpu.CompilerParams(
            collective_id=0, has_side_effects=True, vmem_limit_bytes=62 * 2**20
        ),
        name="reduce_and_step",
    )(activations, proj_block, grad_output, first_moment, second_moment)


def update_kernel(projector_ref, direction_ref, out_ref):
    out_ref[...] = jnp.dot(
        projector_ref[...], direction_ref[...], preferred_element_type=jnp.float32
    ).astype(jnp.bfloat16)


def back_projected(projector, direction):
    rows, rank = projector.shape
    columns = direction.shape[1]
    width = columns // CHUNKS
    return pl.pallas_call(
        update_kernel,
        out_shape=jax.ShapeDtypeStruct((rows, columns), jnp.bfloat16),
        grid=(CHUNKS,),
        in_specs=[
            pl.BlockSpec((rows, rank), lambda i: (0, 0)),
            pl.BlockSpec((rank, width), lambda i: (0, i)),
        ],
        out_specs=pl.BlockSpec((rows, width), lambda i: (0, i)),
        compiler_params=pltpu.CompilerParams(vmem_limit_bytes=40 * 2**20),
        name="back_project",
    )(projector, direction)


def body(activations, grad_output, projector, first_moment, second_moment):
    rank_width = projector.shape[1]
    tp_count = lax.axis_size("tp")
    tp_place = lax.axis_index("tp")
    column_count = rank_width // tp_count
    proj_block = lax.dynamic_slice_in_dim(projector, tp_place * column_count, column_count, 1)
    new_first, new_second, direction = reduced(
        activations, proj_block, grad_output, first_moment, second_moment
    )
    direction_all = lax.all_gather(direction, "fsdp", axis=0, tiled=True)
    return (new_first, new_second, back_projected(projector, direction_all))


def solution(mesh):
    return jax.shard_map(
        body,
        mesh=mesh,
        in_specs=(
            P("fsdp", None),
            P("fsdp", "tp"),
            P("fsdp", None),
            P("fsdp", "tp"),
            P("fsdp", "tp"),
        ),
        out_specs=(P("fsdp", "tp"), P("fsdp", "tp"), P("fsdp", "tp")),
        check_vma=False,
    )
```

```python
import functools

import jax
import jax.numpy as jnp
from jax import lax
from jax.experimental import pallas as pl
from jax.experimental.pallas import tpu as pltpu
from jax.sharding import PartitionSpec as P

first_fix = 0.9999734386011124
second_fix = 0.6339676587267705

MESH = pl.DeviceIdType.MESH
LINE = 4
CORES = 2
CHUNKS = 14
AHEAD = 4
LAG = 4


def reduce_kernel(
    act_ref, proj_ref, grad_ref, first_ref, second_ref,
    new_first_ref, new_second_ref, direction_ref,
    proj_all, acts, acc, acc_in, coords, coords_all, grads, partial, landed, relay,
    line_send, line_recv, row_send, row_recv, act_sem, act_send, act_recv, acc_send, acc_recv,
    coords_send, coords_recv, own_sem, grad_send, grad_recv, part_send, part_recv, relay_recv,
):
    plane = grads.shape[0]
    chips = plane // CORES
    tps = lax.axis_size("tp")
    parts = coords.shape[0]
    depth = proj_ref.shape[0]
    rows = first_ref.shape[0]
    half = first_ref.shape[1] // CORES
    width = half // CHUNKS
    me = lax.axis_index("fsdp")
    tp = lax.axis_index("tp")
    z = lax.div(me, plane)
    slot = lax.rem(me, plane)
    chip = lax.div(slot, CORES)
    core = lax.rem(slot, CORES)
    sibling = chip * CORES + 1 - core

    def in_plane(step):
        return lax.rem(slot + step, plane)

    def on_line(dz, dc):
        return lax.rem(z + dz, LINE), lax.rem(core + dc, CORES)

    low = z < LINE // 2
    middle = jnp.logical_or(z == 1, z == 2)
    partner = jnp.where(low, 1 - z, 5 - z)
    far = jnp.where(low, LINE // 2, 0)
    line_peers = [(dz, dc) for dz in range(LINE) for dc in range(CORES) if dz or dc]

    def device(z_to, slot_to, dt=0):
        return (z_to * plane + slot_to, lax.rem(tp + dt, tps) if dt else tp)

    barrier = pltpu.get_barrier_semaphore()
    for step in range(plane):
        for dt in range(tps):
            if step or dt:
                pl.semaphore_signal(
                    barrier, inc=1, device_id=device(z, in_plane(step), dt), device_id_type=MESH
                )
    for dz, dc in line_peers:
        if dz:
            z_to, core_to = on_line(dz, dc)
            pl.semaphore_signal(
                barrier, inc=1, device_id=device(z_to, chip * CORES + core_to), device_id_type=MESH
            )
    pl.semaphore_wait(barrier, plane * tps - 1 + (LINE - 1) * CORES)

    def arrived(ref, sem):
        pltpu.make_async_copy(ref, ref, sem).wait()

    def line_source(k, way):
        return z + k if way else z - k

    def line_valid(k, way):
        return z + k < LINE if way else z >= k

    def line_next(k, way):
        return jnp.logical_and(line_valid(k, way), z > 0 if way else z < LINE - 1)

    def line_copy(k, way):
        block = line_source(k, way) * chips + chip
        return pltpu.make_async_remote_copy(
            src_ref=proj_all.at[block] if k else proj_ref,
            dst_ref=proj_all.at[block],
            send_sem=line_send.at[way, k],
            recv_sem=line_recv.at[line_source(k, way)],
            device_id=device(z - 1 if way else z + 1, slot),
            device_id_type=MESH,
        )

    def row_copy(z_from, dx, own=False):
        block = z_from * chips + chip
        return pltpu.make_async_remote_copy(
            src_ref=proj_ref if own else proj_all.at[block],
            dst_ref=proj_all.at[block],
            send_sem=row_send.at[dx, z_from],
            recv_sem=row_recv.at[block],
            device_id=device(z, lax.rem(chip + dx, chips) * CORES + core),
            device_id_type=MESH,
        )

    def act_columns(block, side):
        return act_ref.at[:, pl.ds(pl.multiple_of((block * CORES + side) * depth, 128), depth)]

    def act_own(block):
        return pltpu.make_async_copy(act_columns(block, core), acts.at[block, 0], act_sem.at[block])

    def act_copy(block):
        return pltpu.make_async_remote_copy(
            src_ref=act_columns(block, 1 - core),
            dst_ref=acts.at[block, 1],
            send_sem=act_send.at[block],
            recv_sem=act_recv.at[block],
            device_id=device(z, sibling),
            device_id_type=MESH,
        )

    def acc_copy():
        return pltpu.make_async_remote_copy(
            src_ref=acc.at[1],
            dst_ref=acc_in,
            send_sem=acc_send,
            recv_sem=acc_recv,
            device_id=device(z, sibling),
            device_id_type=MESH,
        )

    def coords_place(q):
        place = tp * parts + q
        return lax.rem(place, chips), lax.div(place, chips)

    def coords_copy(q, dc, dt):
        chip_to, block = coords_place(q)
        return pltpu.make_async_remote_copy(
            src_ref=coords.at[q],
            dst_ref=coords_all.at[slot, block],
            send_sem=coords_send.at[q, dc * tps + dt],
            recv_sem=coords_recv.at[slot, block],
            device_id=device(z, chip_to * CORES + lax.rem(core + dc, CORES), dt),
            device_id_type=MESH,
        )

    def each_coords_copy(act):
        for q in range(parts):
            chip_to, _ = coords_place(q)
            for dc in range(CORES):
                for dt in range(tps):
                    if dc or dt:
                        act(coords_copy(q, dc, dt))
                    else:
                        @pl.when(chip_to != chip)
                        def _():
                            act(coords_copy(q, 0, 0))

    def grad_copy(step, i):
        to = in_plane(step)
        start = pl.multiple_of(lax.rem(to, CORES) * half + i * width, 128)
        return pltpu.make_async_remote_copy(
            src_ref=grad_ref.at[:, pl.ds(start, width)],
            dst_ref=grads.at[slot, i],
            send_sem=grad_send.at[step - 1, i],
            recv_sem=grad_recv.at[slot, i],
            device_id=device(z, to),
            device_id_type=MESH,
        )

    def own_copy(i):
        start = pl.multiple_of(core * half + i * width, 128)
        return pltpu.make_async_copy(
            grad_ref.at[:, pl.ds(start, width)], grads.at[slot, i], own_sem.at[i]
        )

    def part_copy(index, i):
        if index == 0:
            z_to, core_to = z, 1 - core
        else:
            z_to, core_to = partner, index - 1
        return pltpu.make_async_remote_copy(
            src_ref=partial.at[z_to * CORES + core_to, i],
            dst_ref=landed.at[core, min(index, 1), i],
            send_sem=part_send.at[index, i],
            recv_sem=part_recv.at[core, min(index, 1), i],
            device_id=device(z_to, chip * CORES + core_to),
            device_id_type=MESH,
        )

    def far_copy(f, core_to, i, relayed):
        if relayed:
            dst_ref, recv_sem = landed.at[core, 2, i], part_recv.at[core, 2, i]
            target = device(far + f, chip * CORES + core_to)
        else:
            dst_ref, recv_sem = relay.at[f, core_to, i], relay_recv.at[f, core_to, i]
            target = device(partner, slot)
        return pltpu.make_async_remote_copy(
            src_ref=partial.at[(far + f) * CORES + core_to, i],
            dst_ref=dst_ref,
            send_sem=part_send.at[3 + f * CORES + core_to, i],
            recv_sem=recv_sem,
            device_id=target,
            device_id_type=MESH,
        )

    far_blocks = [(f, core_to) for f in range(LINE // 2) for core_to in range(CORES)]

    def send_grads(i):
        own_copy(i).start()
        for step in range(1, plane):
            grad_copy(step, i).start()

    blocks = acts.shape[0]
    for way in range(2):
        @pl.when(line_next(0, way))
        def _():
            line_copy(0, way).start()

    for dx in range(1, chips):
        row_copy(z, dx, True).start()
    for block in range(blocks):
        act_own(block).start()
        act_copy(block).start()
    acc[...] = jnp.zeros_like(acc)

    def accumulate(block, features):
        act_own(block).wait()
        arrived(acts.at[block, 1], act_recv.at[block])
        tokens = acts.shape[2]
        both = acts[block].reshape(CORES * tokens, depth)
        acc[...] += jnp.dot(both, features, preferred_element_type=jnp.float32).reshape(acc.shape)

    accumulate(z * chips + chip, proj_ref[...])
    for k in range(1, LINE):
        for way in range(2):
            @pl.when(line_valid(k, way))
            def _():
                z_from = line_source(k, way)
                arrived(proj_all.at[z_from * chips + chip], line_recv.at[z_from])
                for dx in range(1, chips):
                    row_copy(z_from, dx).start()

            if k < LINE - 1:
                @pl.when(line_next(k, way))
                def _():
                    line_copy(k, way).start()

        for way in range(2):
            @pl.when(line_valid(k, way))
            def _():
                block = line_source(k, way) * chips + chip
                accumulate(block, proj_all[block])

    send_grads(0)
    for dz in range(LINE):
        z_from, _ = on_line(dz, 0)
        for dx in range(1, chips):
            block = z_from * chips + lax.rem(chip + dx, chips)
            arrived(proj_all.at[block], row_recv.at[block])
            accumulate(block, proj_all[block])
    acc_copy().start()
    send_grads(1)
    arrived(acc_in, acc_recv)
    summed = jnp.transpose(acc[0] + acc_in[...]).astype(jnp.bfloat16)
    coords[...] = summed.reshape(coords.shape)
    each_coords_copy(lambda copy: copy.start())
    for q in range(parts):
        chip_to, own_block = coords_place(q)

        @pl.when(chip_to == chip)
        def _():
            coords_all[slot, own_block] = coords[q]

    for step in range(plane):
        source = in_plane(step)
        for block in range(LINE):
            if step:
                arrived(coords_all.at[source, block], coords_recv.at[source, block])
            else:
                @pl.when(lax.div(block * chips + chip, parts) != tp)
                def _():
                    arrived(coords_all.at[source, block], coords_recv.at[source, block])

    for i in range(2, AHEAD):
        send_grads(i)

    def multiply(i):
        own_copy(i).wait()
        for step in range(1, plane):
            source = in_plane(step)
            arrived(grads.at[source, i], grad_recv.at[source, i])
        total = 0.0
        for source in range(plane):
            ranks = coords_all[source].reshape(LINE * CORES * rows, -1)
            total += jnp.dot(ranks, grads[source, i], preferred_element_type=jnp.float32)
        total = total.astype(jnp.bfloat16)
        for block in range(LINE * CORES):
            partial[block, i] = total[block * rows : (block + 1) * rows]
        for index in range(1 + CORES):
            part_copy(index, i).start()
        landed[core, 0, i] = partial[z * CORES + core, i]

        @pl.when(jnp.logical_not(middle))
        def _():
            for f, core_to in far_blocks:
                far_copy(f, core_to, i, False).start()

    def pass_on(i):
        @pl.when(middle)
        def _():
            for f, core_to in far_blocks:
                arrived(relay.at[f, core_to, i], relay_recv.at[f, core_to, i])
                block = (far + f) * CORES + core_to
                both = partial[block, i].astype(jnp.float32) + relay[f, core_to, i].astype(jnp.float32)
                partial[block, i] = both.astype(jnp.bfloat16)
                far_copy(f, core_to, i, True).start()

    def adam(i):
        for dc in range(CORES):
            core_from = lax.rem(core + dc, CORES)
            for place in range(0 if dc else 1, 3):
                arrived(landed.at[core_from, place, i], part_recv.at[core_from, place, i])
        for side in range(CORES):
            lowrank = landed[side, 0, i].astype(jnp.float32)
            for place in range(1, 3):
                lowrank += landed[side, place, i].astype(jnp.float32)
            columns = pl.ds(pl.multiple_of(side * half + i * width, 128), width)
            new_first = 0.9 * first_ref[:, columns] + 0.1 * lowrank
            new_second = 0.99 * second_ref[:, columns] + 0.01 * lowrank * lowrank
            new_first_ref[:, columns] = new_first
            new_second_ref[:, columns] = new_second
            direction_ref[:, columns] = (
                new_first / first_fix / (jnp.sqrt(new_second / second_fix) + 1e-08)
            ).astype(jnp.bfloat16)

    @pl.loop(0, CHUNKS)
    def _(i):
        @pl.when(i + AHEAD < CHUNKS)
        def _():
            send_grads(i + AHEAD)

        multiply(i)

        @pl.when(i >= 1)
        def _():
            pass_on(i - 1)

        @pl.when(i >= LAG)
        def _():
            adam(i - LAG)

    pass_on(CHUNKS - 1)

    @pl.loop(CHUNKS - LAG, CHUNKS)
    def _(i):
        adam(i)

    for k in range(LINE - 1):
        for way in range(2):
            @pl.when(line_next(k, way))
            def _():
                line_copy(k, way).wait_send()

    for z_from in range(LINE):
        for dx in range(1, chips):
            row_copy(z_from, dx).wait_send()
    for block in range(blocks):
        act_copy(block).wait_send()
    acc_copy().wait_send()
    each_coords_copy(lambda copy: copy.wait_send())

    @pl.loop(0, CHUNKS)
    def _(i):
        for step in range(1, plane):
            grad_copy(step, i).wait_send()
        for index in range(1 + CORES):
            part_copy(index, i).wait_send()
        for f, core_to in far_blocks:
            far_copy(f, core_to, i, True).wait_send()


def reduced(activations, proj_block, grad_output, first_moment, second_moment):
    tps = lax.axis_size("tp")
    plane = lax.axis_size("fsdp") // LINE
    blocks = plane * LINE // CORES
    tokens = activations.shape[0]
    depth, ranks = proj_block.shape
    rows, columns = first_moment.shape
    parts = ranks // (CORES * rows)
    width = columns // CORES // CHUNKS
    peers = LINE * CORES - 1
    dma = pltpu.SemaphoreType.DMA
    vmem = pl.BlockSpec(memory_space=pltpu.VMEM)
    hbm = pl.BlockSpec(memory_space=pl.ANY)
    return pl.pallas_call(
        reduce_kernel,
        out_shape=(
            jax.ShapeDtypeStruct((rows, columns), jnp.float32),
            jax.ShapeDtypeStruct((rows, columns), jnp.float32),
            jax.ShapeDtypeStruct((rows, columns), jnp.bfloat16),
        ),
        in_specs=[hbm, vmem, hbm, vmem, vmem],
        out_specs=(vmem, vmem, vmem),
        scratch_shapes=[
            pltpu.VMEM((blocks, depth, ranks), jnp.bfloat16),
            pltpu.VMEM((blocks, CORES, tokens, depth), jnp.bfloat16),
            pltpu.VMEM((CORES, tokens, ranks), jnp.float32),
            pltpu.VMEM((tokens, ranks), jnp.float32),
            pltpu.VMEM((parts, CORES * rows, tokens), jnp.bfloat16),
            pltpu.VMEM((plane, LINE, CORES * rows, tokens), jnp.bfloat16),
            pltpu.VMEM((plane, CHUNKS, tokens, width), jnp.bfloat16),
            pltpu.VMEM((LINE * CORES, CHUNKS, rows, width), jnp.bfloat16),
            pltpu.VMEM((CORES, 3, CHUNKS, rows, width), jnp.bfloat16),
            pltpu.VMEM((LINE // 2, CORES, CHUNKS, rows, width), jnp.bfloat16),
            dma((2, LINE - 1)),
            dma((LINE,)),
            dma((plane // CORES, LINE)),
            dma((blocks,)),
            dma((blocks,)),
            dma((blocks,)),
            dma((blocks,)),
            dma,
            dma,
            dma((parts, CORES * tps)),
            dma((plane, LINE)),
            dma((CHUNKS,)),
            dma((plane - 1, CHUNKS)),
            dma((plane, CHUNKS)),
            dma((peers, CHUNKS)),
            dma((CORES, 3, CHUNKS)),
            dma((LINE // 2, CORES, CHUNKS)),
        ],
        compiler_params=pltpu.CompilerParams(
            collective_id=0, has_side_effects=True, vmem_limit_bytes=62 * 2**20
        ),
        name="reduce_and_step",
    )(activations, proj_block, grad_output, first_moment, second_moment)


def update_kernel(projector_ref, direction_ref, out_ref):
    out_ref[...] = jnp.dot(
        projector_ref[...], direction_ref[...], preferred_element_type=jnp.float32
    ).astype(jnp.bfloat16)


def back_projected(projector, direction):
    rows, rank = projector.shape
    columns = direction.shape[1]
    width = columns // CHUNKS
    return pl.pallas_call(
        update_kernel,
        out_shape=jax.ShapeDtypeStruct((rows, columns), jnp.bfloat16),
        grid=(CHUNKS,),
        in_specs=[
            pl.BlockSpec((rows, rank), lambda i: (0, 0)),
            pl.BlockSpec((rank, width), lambda i: (0, i)),
        ],
        out_specs=pl.BlockSpec((rows, width), lambda i: (0, i)),
        compiler_params=pltpu.CompilerParams(vmem_limit_bytes=40 * 2**20),
        name="back_project",
    )(projector, direction)


def body(activations, grad_output, projector, first_moment, second_moment):
    rank_width = projector.shape[1]
    tp_count = lax.axis_size("tp")
    tp_place = lax.axis_index("tp")
    column_count = rank_width // tp_count
    proj_block = lax.dynamic_slice_in_dim(projector, tp_place * column_count, column_count, 1)
    new_first, new_second, direction = reduced(
        activations, proj_block, grad_output, first_moment, second_moment
    )
    direction_all = lax.all_gather(direction, "fsdp", axis=0, tiled=True)
    return (new_first, new_second, back_projected(projector, direction_all))


def solution(mesh):
    return jax.shard_map(
        body,
        mesh=mesh,
        in_specs=(
            P("fsdp", None),
            P("fsdp", "tp"),
            P("fsdp", None),
            P("fsdp", "tp"),
            P("fsdp", "tp"),
        ),
        out_specs=(P("fsdp", "tp"), P("fsdp", "tp"), P("fsdp", "tp")),
        check_vma=False,
    )
```

```python
import functools

import jax
import jax.numpy as jnp
from jax import lax
from jax.experimental import pallas as pl
from jax.experimental.pallas import tpu as pltpu
from jax.sharding import PartitionSpec as P

first_fix = 0.9999734386011124
second_fix = 0.6339676587267705

MESH = pl.DeviceIdType.MESH
LINE = 4
CORES = 2
CHUNKS = 14
AHEAD = 6
REACH = 2
LAG = 4


def reduce_kernel(
    act_ref, proj_ref, grad_ref, first_ref, second_ref,
    lowrank_ref, direction_ref,
    proj_all, acts, acc, acc_in, coords, coords_all, grads, partial, landed, relay,
    line_send, line_recv, cross_send, row_send, row_recv, act_sem, act_send, act_recv, acc_send, acc_recv,
    coords_send, coords_recv, own_sem, grad_send, grad_recv, part_send, part_recv, relay_recv,
):
    plane = grads.shape[0]
    chips = plane // CORES
    tps = lax.axis_size("tp")
    parts = coords.shape[0]
    depth = proj_ref.shape[0]
    rows = first_ref.shape[0]
    half = first_ref.shape[1] // CORES
    width = half // CHUNKS
    me = lax.axis_index("fsdp")
    tp = lax.axis_index("tp")
    z = lax.div(me, plane)
    slot = lax.rem(me, plane)
    chip = lax.div(slot, CORES)
    core = lax.rem(slot, CORES)
    sibling = chip * CORES + 1 - core

    def in_plane(step):
        return lax.rem(slot + step, plane)

    def on_line(dz, dc):
        return lax.rem(z + dz, LINE), lax.rem(core + dc, CORES)

    low = z < LINE // 2
    middle = jnp.logical_or(z == 1, z == 2)
    partner = jnp.where(low, 1 - z, 5 - z)
    far = jnp.where(low, LINE // 2, 0)
    line_peers = [(dz, dc) for dz in range(LINE) for dc in range(CORES) if dz or dc]

    def device(z_to, slot_to, dt=0):
        return (z_to * plane + slot_to, lax.rem(tp + dt, tps) if dt else tp)

    barrier = pltpu.get_barrier_semaphore()
    for step in range(plane):
        for dt in range(tps):
            if step or dt:
                pl.semaphore_signal(
                    barrier, inc=1, device_id=device(z, in_plane(step), dt), device_id_type=MESH
                )
    for dz, dc in line_peers:
        if dz:
            z_to, core_to = on_line(dz, dc)
            pl.semaphore_signal(
                barrier, inc=1, device_id=device(z_to, chip * CORES + core_to), device_id_type=MESH
            )
    pl.semaphore_wait(barrier, plane * tps - 1 + (LINE - 1) * CORES)

    def arrived(ref, sem):
        pltpu.make_async_copy(ref, ref, sem).wait()

    def line_source(k, way):
        return z + k if way else z - k

    def line_valid(k, way):
        return z + k < LINE if way else z >= k

    def line_next(k, way):
        return jnp.logical_and(line_valid(k, way), z > 0 if way else z < LINE - 1)

    def line_copy(k, way):
        block = line_source(k, way) * chips + chip
        return pltpu.make_async_remote_copy(
            src_ref=proj_all.at[block] if k else proj_ref,
            dst_ref=proj_all.at[block],
            send_sem=line_send.at[way, k],
            recv_sem=line_recv.at[line_source(k, way)],
            device_id=device(z - 1 if way else z + 1, slot),
            device_id_type=MESH,
        )

    def row_copy(z_from, dx, own=False):
        block = z_from * chips + chip
        return pltpu.make_async_remote_copy(
            src_ref=proj_ref if own else proj_all.at[block],
            dst_ref=proj_all.at[block],
            send_sem=row_send.at[dx, z_from],
            recv_sem=row_recv.at[block],
            device_id=device(z, lax.rem(chip + dx, chips) * CORES + core),
            device_id_type=MESH,
        )

    def cross_copy(k, way, dx):
        block = line_source(k, way) * chips + lax.rem(chip + dx, chips)
        return pltpu.make_async_remote_copy(
            src_ref=proj_all.at[block],
            dst_ref=proj_all.at[block],
            send_sem=cross_send.at[way, k, dx],
            recv_sem=row_recv.at[block],
            device_id=device(z - 1 if way else z + 1, slot),
            device_id_type=MESH,
        )

    def act_columns(block, side):
        return act_ref.at[:, pl.ds(pl.multiple_of((block * CORES + side) * depth, 128), depth)]

    def act_own(block):
        return pltpu.make_async_copy(act_columns(block, core), acts.at[block, 0], act_sem.at[block])

    def act_copy(block):
        return pltpu.make_async_remote_copy(
            src_ref=act_columns(block, 1 - core),
            dst_ref=acts.at[block, 1],
            send_sem=act_send.at[block],
            recv_sem=act_recv.at[block],
            device_id=device(z, sibling),
            device_id_type=MESH,
        )

    def acc_copy():
        return pltpu.make_async_remote_copy(
            src_ref=acc.at[1],
            dst_ref=acc_in,
            send_sem=acc_send,
            recv_sem=acc_recv,
            device_id=device(z, sibling),
            device_id_type=MESH,
        )

    def coords_place(q):
        place = tp * parts + q
        return lax.rem(place, chips), lax.div(place, chips)

    def coords_copy(q, dc, dt):
        chip_to, block = coords_place(q)
        return pltpu.make_async_remote_copy(
            src_ref=coords.at[q],
            dst_ref=coords_all.at[slot, block],
            send_sem=coords_send.at[q, dc * tps + dt],
            recv_sem=coords_recv.at[slot, block],
            device_id=device(z, chip_to * CORES + lax.rem(core + dc, CORES), dt),
            device_id_type=MESH,
        )

    def each_coords_copy(act):
        for q in range(parts):
            chip_to, _ = coords_place(q)
            for dc in range(CORES):
                for dt in range(tps):
                    if dc or dt:
                        act(coords_copy(q, dc, dt))
                    else:
                        @pl.when(chip_to != chip)
                        def _():
                            act(coords_copy(q, 0, 0))

    def grad_copy(step, i):
        to = in_plane(step)
        start = pl.multiple_of(lax.rem(to, CORES) * half + i * width, 128)
        return pltpu.make_async_remote_copy(
            src_ref=grad_ref.at[:, pl.ds(start, width)],
            dst_ref=grads.at[slot, i],
            send_sem=grad_send.at[step - 1, i],
            recv_sem=grad_recv.at[slot, i],
            device_id=device(z, to),
            device_id_type=MESH,
        )

    def own_copy(i):
        start = pl.multiple_of(core * half + i * width, 128)
        return pltpu.make_async_copy(
            grad_ref.at[:, pl.ds(start, width)], grads.at[slot, i], own_sem.at[i]
        )

    def part_copy(index, i):
        if index == 0:
            z_to, core_to = z, 1 - core
        else:
            z_to, core_to = partner, index - 1
        return pltpu.make_async_remote_copy(
            src_ref=partial.at[z_to * CORES + core_to, i],
            dst_ref=landed.at[core, min(index, 1), i],
            send_sem=part_send.at[index, i],
            recv_sem=part_recv.at[core, min(index, 1), i],
            device_id=device(z_to, chip * CORES + core_to),
            device_id_type=MESH,
        )

    def far_copy(f, core_to, i, relayed):
        if relayed:
            dst_ref, recv_sem = landed.at[core, 2, i], part_recv.at[core, 2, i]
            target = device(far + f, chip * CORES + core_to)
        else:
            dst_ref, recv_sem = relay.at[f, core_to, i], relay_recv.at[f, core_to, i]
            target = device(partner, slot)
        return pltpu.make_async_remote_copy(
            src_ref=partial.at[(far + f) * CORES + core_to, i],
            dst_ref=dst_ref,
            send_sem=part_send.at[3 + f * CORES + core_to, i],
            recv_sem=recv_sem,
            device_id=target,
            device_id_type=MESH,
        )

    far_blocks = [(f, core_to) for f in range(LINE // 2) for core_to in range(CORES)]

    def send_grads(i):
        own_copy(i).start()
        for step in range(1, plane):
            grad_copy(step, i).start()

    blocks = acts.shape[0]
    for way in range(2):
        @pl.when(line_next(0, way))
        def _():
            line_copy(0, way).start()

    for dx in range(1, chips):
        row_copy(z, dx, True).start()
    for block in range(blocks):
        act_own(block).start()
        act_copy(block).start()
    acc[...] = jnp.zeros_like(acc)

    def accumulate(block, features):
        act_own(block).wait()
        arrived(acts.at[block, 1], act_recv.at[block])
        tokens = acts.shape[2]
        both = acts[block].reshape(CORES * tokens, depth)
        acc[...] += jnp.dot(both, features, preferred_element_type=jnp.float32).reshape(acc.shape)

    def take_beside(k, way):
        for dx in range(1, chips):
            block = line_source(k, way) * chips + lax.rem(chip + dx, chips)
            arrived(proj_all.at[block], row_recv.at[block])
            if k < REACH:
                for onward in range(2) if k == 0 else (way,):
                    @pl.when(line_next(k, onward))
                    def _():
                        cross_copy(k, onward, dx).start()

            accumulate(block, proj_all[block])

    accumulate(z * chips + chip, proj_ref[...])
    take_beside(0, 0)
    send_grads(0)
    for k in range(1, LINE):
        for way in range(2):
            @pl.when(line_valid(k, way))
            def _():
                z_from = line_source(k, way)
                arrived(proj_all.at[z_from * chips + chip], line_recv.at[z_from])
                if k > REACH:
                    for dx in range(1, chips):
                        row_copy(z_from, dx).start()

            if k < LINE - 1:
                @pl.when(line_next(k, way))
                def _():
                    line_copy(k, way).start()

        for way in range(2):
            @pl.when(line_valid(k, way))
            def _():
                if k <= REACH:
                    take_beside(k, way)
                block = line_source(k, way) * chips + chip
                accumulate(block, proj_all[block])

        if k < LINE - 1:
            send_grads(k)
    for k in range(REACH + 1, LINE):
        for way in range(2):
            @pl.when(line_valid(k, way))
            def _():
                take_beside(k, way)

    send_grads(LINE - 1)
    acc_copy().start()
    arrived(acc_in, acc_recv)
    summed = jnp.transpose(acc[0] + acc_in[...]).astype(jnp.bfloat16)
    coords[...] = summed.reshape(coords.shape)
    each_coords_copy(lambda copy: copy.start())
    for q in range(parts):
        chip_to, own_block = coords_place(q)

        @pl.when(chip_to == chip)
        def _():
            coords_all[slot, own_block] = coords[q]

    for step in range(plane):
        source = in_plane(step)
        for block in range(LINE):
            if step:
                arrived(coords_all.at[source, block], coords_recv.at[source, block])
            else:
                @pl.when(lax.div(block * chips + chip, parts) != tp)
                def _():
                    arrived(coords_all.at[source, block], coords_recv.at[source, block])

    for i in range(LINE, AHEAD):
        send_grads(i)

    def multiply(i):
        own_copy(i).wait()
        for step in range(1, plane):
            source = in_plane(step)
            arrived(grads.at[source, i], grad_recv.at[source, i])
        total = 0.0
        for source in range(plane):
            ranks = coords_all[source].reshape(LINE * CORES * rows, -1)
            total += jnp.dot(ranks, grads[source, i], preferred_element_type=jnp.float32)
        total = total.astype(jnp.bfloat16)
        for block in range(LINE * CORES):
            partial[block, i] = total[block * rows : (block + 1) * rows]
        for index in range(1 + CORES):
            part_copy(index, i).start()
        landed[core, 0, i] = partial[z * CORES + core, i]

        @pl.when(jnp.logical_not(middle))
        def _():
            for f, core_to in far_blocks:
                far_copy(f, core_to, i, False).start()

    def pass_on(i):
        @pl.when(middle)
        def _():
            for f, core_to in far_blocks:
                arrived(relay.at[f, core_to, i], relay_recv.at[f, core_to, i])
                block = (far + f) * CORES + core_to
                both = partial[block, i].astype(jnp.float32) + relay[f, core_to, i].astype(jnp.float32)
                partial[block, i] = both.astype(jnp.bfloat16)
                far_copy(f, core_to, i, True).start()

    def adam(i):
        for dc in range(CORES):
            core_from = lax.rem(core + dc, CORES)
            for place in range(0 if dc else 1, 3):
                arrived(landed.at[core_from, place, i], part_recv.at[core_from, place, i])
        for side in range(CORES):
            lowrank = landed[side, 0, i].astype(jnp.float32)
            for place in range(1, 3):
                lowrank += landed[side, place, i].astype(jnp.float32)
            columns = pl.ds(pl.multiple_of(side * half + i * width, 128), width)
            new_first = 0.9 * first_ref[:, columns] + 0.1 * lowrank
            new_second = 0.99 * second_ref[:, columns] + 0.01 * lowrank * lowrank
            lowrank_ref[:, columns] = lowrank
            direction_ref[:, columns] = (
                new_first / first_fix / (jnp.sqrt(new_second / second_fix) + 1e-08)
            ).astype(jnp.bfloat16)

    @pl.loop(0, CHUNKS)
    def _(i):
        @pl.when(i + AHEAD < CHUNKS)
        def _():
            send_grads(i + AHEAD)

        multiply(i)

        @pl.when(i >= 1)
        def _():
            pass_on(i - 1)

        @pl.when(i >= LAG)
        def _():
            adam(i - LAG)

    pass_on(CHUNKS - 1)

    @pl.loop(CHUNKS - LAG, CHUNKS)
    def _(i):
        adam(i)

    for k in range(LINE - 1):
        for way in range(2):
            @pl.when(line_next(k, way))
            def _():
                line_copy(k, way).wait_send()

    for dx in range(1, chips):
        row_copy(z, dx, True).wait_send()
    for k in range(REACH):
        for way in range(2):
            @pl.when(line_next(k, way))
            def _():
                for dx in range(1, chips):
                    cross_copy(k, way, dx).wait_send()

    for k in range(REACH + 1, LINE):
        for way in range(2):
            @pl.when(line_valid(k, way))
            def _():
                for dx in range(1, chips):
                    row_copy(line_source(k, way), dx).wait_send()

    for block in range(blocks):
        act_copy(block).wait_send()
    acc_copy().wait_send()
    each_coords_copy(lambda copy: copy.wait_send())

    @pl.loop(0, CHUNKS)
    def _(i):
        for step in range(1, plane):
            grad_copy(step, i).wait_send()
        for index in range(1 + CORES):
            part_copy(index, i).wait_send()
        for f, core_to in far_blocks:
            far_copy(f, core_to, i, True).wait_send()


def reduced(activations, proj_block, grad_output, first_moment, second_moment):
    tps = lax.axis_size("tp")
    plane = lax.axis_size("fsdp") // LINE
    blocks = plane * LINE // CORES
    tokens = activations.shape[0]
    depth, ranks = proj_block.shape
    rows, columns = first_moment.shape
    parts = ranks // (CORES * rows)
    width = columns // CORES // CHUNKS
    peers = LINE * CORES - 1
    dma = pltpu.SemaphoreType.DMA
    vmem = pl.BlockSpec(memory_space=pltpu.VMEM)
    hbm = pl.BlockSpec(memory_space=pl.ANY)
    return pl.pallas_call(
        reduce_kernel,
        out_shape=(
            jax.ShapeDtypeStruct((rows, columns), jnp.float32),
            jax.ShapeDtypeStruct((rows, columns), jnp.bfloat16),
        ),
        in_specs=[hbm, vmem, hbm, vmem, vmem],
        out_specs=(vmem, vmem),
        scratch_shapes=[
            pltpu.VMEM((blocks, depth, ranks), jnp.bfloat16),
            pltpu.VMEM((blocks, CORES, tokens, depth), jnp.bfloat16),
            pltpu.VMEM((CORES, tokens, ranks), jnp.float32),
            pltpu.VMEM((tokens, ranks), jnp.float32),
            pltpu.VMEM((parts, CORES * rows, tokens), jnp.bfloat16),
            pltpu.VMEM((plane, LINE, CORES * rows, tokens), jnp.bfloat16),
            pltpu.VMEM((plane, CHUNKS, tokens, width), jnp.bfloat16),
            pltpu.VMEM((LINE * CORES, CHUNKS, rows, width), jnp.bfloat16),
            pltpu.VMEM((CORES, 3, CHUNKS, rows, width), jnp.bfloat16),
            pltpu.VMEM((LINE // 2, CORES, CHUNKS, rows, width), jnp.bfloat16),
            dma((2, LINE - 1)),
            dma((LINE,)),
            dma((2, REACH, plane // CORES)),
            dma((plane // CORES, LINE)),
            dma((blocks,)),
            dma((blocks,)),
            dma((blocks,)),
            dma((blocks,)),
            dma,
            dma,
            dma((parts, CORES * tps)),
            dma((plane, LINE)),
            dma((CHUNKS,)),
            dma((plane - 1, CHUNKS)),
            dma((plane, CHUNKS)),
            dma((peers, CHUNKS)),
            dma((CORES, 3, CHUNKS)),
            dma((LINE // 2, CORES, CHUNKS)),
        ],
        compiler_params=pltpu.CompilerParams(
            collective_id=0, has_side_effects=True, vmem_limit_bytes=62 * 2**20
        ),
        name="reduce_and_step",
    )(activations, proj_block, grad_output, first_moment, second_moment)


def update_kernel(projector_ref, direction_ref, out_ref):
    out_ref[...] = jnp.dot(
        projector_ref[...], direction_ref[...], preferred_element_type=jnp.float32
    ).astype(jnp.bfloat16)


def back_projected(projector, direction):
    rows, rank = projector.shape
    columns = direction.shape[1]
    width = columns // CHUNKS
    return pl.pallas_call(
        update_kernel,
        out_shape=jax.ShapeDtypeStruct((rows, columns), jnp.bfloat16),
        grid=(CHUNKS,),
        in_specs=[
            pl.BlockSpec((rows, rank), lambda i: (0, 0)),
            pl.BlockSpec((rank, width), lambda i: (0, i)),
        ],
        out_specs=pl.BlockSpec((rows, width), lambda i: (0, i)),
        compiler_params=pltpu.CompilerParams(vmem_limit_bytes=40 * 2**20),
        name="back_project",
    )(projector, direction)


def body(activations, grad_output, projector, first_moment, second_moment):
    rank_width = projector.shape[1]
    tp_count = lax.axis_size("tp")
    tp_place = lax.axis_index("tp")
    column_count = rank_width // tp_count
    proj_block = lax.dynamic_slice_in_dim(projector, tp_place * column_count, column_count, 1)
    lowrank, direction = reduced(
        activations, proj_block, grad_output, first_moment, second_moment
    )
    new_first = 0.9 * first_moment + 0.1 * lowrank
    new_second = 0.99 * second_moment + 0.01 * lowrank * lowrank
    direction_all = lax.all_gather(direction, "fsdp", axis=0, tiled=True)
    return (new_first, new_second, back_projected(projector, direction_all))


def solution(mesh):
    return jax.shard_map(
        body,
        mesh=mesh,
        in_specs=(
            P("fsdp", None),
            P("fsdp", "tp"),
            P("fsdp", None),
            P("fsdp", "tp"),
            P("fsdp", "tp"),
        ),
        out_specs=(P("fsdp", "tp"), P("fsdp", "tp"), P("fsdp", "tp")),
        check_vma=False,
    )
```

```python
import functools

import jax
import jax.numpy as jnp
from jax import lax
from jax.experimental import pallas as pl
from jax.experimental.pallas import tpu as pltpu
from jax.sharding import PartitionSpec as P

first_fix = 0.9999734386011124
second_fix = 0.6339676587267705

MESH = pl.DeviceIdType.MESH
LINE = 4
CORES = 2
CHUNKS = 14
AHEAD = 6
REACH = 2
LAG = 4


def reduce_kernel(
    act_ref, proj_ref, grad_ref, first_in, second_in,
    lowrank_ref, direction_ref,
    proj_all, acts, acc, acc_in, coords, coords_all, grads, partial, landed, relay,
    first_ref, second_ref, moment_sem,
    line_send, line_recv, cross_send, row_send, row_recv, act_sem, act_send, act_recv, acc_send, acc_recv,
    coords_send, coords_recv, own_sem, grad_send, grad_recv, part_send, part_recv, relay_recv,
):
    plane = grads.shape[0]
    chips = plane // CORES
    tps = lax.axis_size("tp")
    parts = coords.shape[0]
    depth = proj_ref.shape[0]
    rows = first_ref.shape[0]
    half = first_ref.shape[1] // CORES
    width = half // CHUNKS
    me = lax.axis_index("fsdp")
    tp = lax.axis_index("tp")
    z = lax.div(me, plane)
    slot = lax.rem(me, plane)
    chip = lax.div(slot, CORES)
    core = lax.rem(slot, CORES)
    sibling = chip * CORES + 1 - core

    def in_plane(step):
        return lax.rem(slot + step, plane)

    def on_line(dz, dc):
        return lax.rem(z + dz, LINE), lax.rem(core + dc, CORES)

    low = z < LINE // 2
    middle = jnp.logical_or(z == 1, z == 2)
    partner = jnp.where(low, 1 - z, 5 - z)
    far = jnp.where(low, LINE // 2, 0)
    line_peers = [(dz, dc) for dz in range(LINE) for dc in range(CORES) if dz or dc]

    def device(z_to, slot_to, dt=0):
        return (z_to * plane + slot_to, lax.rem(tp + dt, tps) if dt else tp)

    barrier = pltpu.get_barrier_semaphore()
    for step in range(plane):
        for dt in range(tps):
            if step or dt:
                pl.semaphore_signal(
                    barrier, inc=1, device_id=device(z, in_plane(step), dt), device_id_type=MESH
                )
    for dz, dc in line_peers:
        if dz:
            z_to, core_to = on_line(dz, dc)
            pl.semaphore_signal(
                barrier, inc=1, device_id=device(z_to, chip * CORES + core_to), device_id_type=MESH
            )
    pl.semaphore_wait(barrier, plane * tps - 1 + (LINE - 1) * CORES)

    def arrived(ref, sem):
        pltpu.make_async_copy(ref, ref, sem).wait()

    def line_source(k, way):
        return z + k if way else z - k

    def line_valid(k, way):
        return z + k < LINE if way else z >= k

    def line_next(k, way):
        return jnp.logical_and(line_valid(k, way), z > 0 if way else z < LINE - 1)

    def line_copy(k, way):
        block = line_source(k, way) * chips + chip
        return pltpu.make_async_remote_copy(
            src_ref=proj_all.at[block] if k else proj_ref,
            dst_ref=proj_all.at[block],
            send_sem=line_send.at[way, k],
            recv_sem=line_recv.at[line_source(k, way)],
            device_id=device(z - 1 if way else z + 1, slot),
            device_id_type=MESH,
        )

    def row_copy(z_from, dx, own=False):
        block = z_from * chips + chip
        return pltpu.make_async_remote_copy(
            src_ref=proj_ref if own else proj_all.at[block],
            dst_ref=proj_all.at[block],
            send_sem=row_send.at[dx, z_from],
            recv_sem=row_recv.at[block],
            device_id=device(z, lax.rem(chip + dx, chips) * CORES + core),
            device_id_type=MESH,
        )

    def cross_copy(k, way, dx):
        block = line_source(k, way) * chips + lax.rem(chip + dx, chips)
        return pltpu.make_async_remote_copy(
            src_ref=proj_all.at[block],
            dst_ref=proj_all.at[block],
            send_sem=cross_send.at[way, k, dx],
            recv_sem=row_recv.at[block],
            device_id=device(z - 1 if way else z + 1, slot),
            device_id_type=MESH,
        )

    def act_columns(block, side):
        return act_ref.at[:, pl.ds(pl.multiple_of((block * CORES + side) * depth, 128), depth)]

    def act_own(block):
        return pltpu.make_async_copy(act_columns(block, core), acts.at[block, 0], act_sem.at[block])

    def act_copy(block):
        return pltpu.make_async_remote_copy(
            src_ref=act_columns(block, 1 - core),
            dst_ref=acts.at[block, 1],
            send_sem=act_send.at[block],
            recv_sem=act_recv.at[block],
            device_id=device(z, sibling),
            device_id_type=MESH,
        )

    def acc_copy():
        return pltpu.make_async_remote_copy(
            src_ref=acc.at[1],
            dst_ref=acc_in,
            send_sem=acc_send,
            recv_sem=acc_recv,
            device_id=device(z, sibling),
            device_id_type=MESH,
        )

    def coords_place(q):
        place = tp * parts + q
        return lax.rem(place, chips), lax.div(place, chips)

    def coords_copy(q, dc, dt):
        chip_to, block = coords_place(q)
        return pltpu.make_async_remote_copy(
            src_ref=coords.at[q],
            dst_ref=coords_all.at[slot, block],
            send_sem=coords_send.at[q, dc * tps + dt],
            recv_sem=coords_recv.at[slot, block],
            device_id=device(z, chip_to * CORES + lax.rem(core + dc, CORES), dt),
            device_id_type=MESH,
        )

    def each_coords_copy(act):
        for q in range(parts):
            chip_to, _ = coords_place(q)
            for dc in range(CORES):
                for dt in range(tps):
                    if dc or dt:
                        act(coords_copy(q, dc, dt))
                    else:
                        @pl.when(chip_to != chip)
                        def _():
                            act(coords_copy(q, 0, 0))

    def grad_copy(step, i):
        to = in_plane(step)
        start = pl.multiple_of(lax.rem(to, CORES) * half + i * width, 128)
        return pltpu.make_async_remote_copy(
            src_ref=grad_ref.at[:, pl.ds(start, width)],
            dst_ref=grads.at[slot, i],
            send_sem=grad_send.at[step - 1, i],
            recv_sem=grad_recv.at[slot, i],
            device_id=device(z, to),
            device_id_type=MESH,
        )

    def own_copy(i):
        start = pl.multiple_of(core * half + i * width, 128)
        return pltpu.make_async_copy(
            grad_ref.at[:, pl.ds(start, width)], grads.at[slot, i], own_sem.at[i]
        )

    def part_copy(index, i):
        if index == 0:
            z_to, core_to = z, 1 - core
        else:
            z_to, core_to = partner, index - 1
        return pltpu.make_async_remote_copy(
            src_ref=partial.at[z_to * CORES + core_to, i],
            dst_ref=landed.at[core, min(index, 1), i],
            send_sem=part_send.at[index, i],
            recv_sem=part_recv.at[core, min(index, 1), i],
            device_id=device(z_to, chip * CORES + core_to),
            device_id_type=MESH,
        )

    def far_copy(f, core_to, i, relayed):
        if relayed:
            dst_ref, recv_sem = landed.at[core, 2, i], part_recv.at[core, 2, i]
            target = device(far + f, chip * CORES + core_to)
        else:
            dst_ref, recv_sem = relay.at[f, core_to, i], relay_recv.at[f, core_to, i]
            target = device(partner, slot)
        return pltpu.make_async_remote_copy(
            src_ref=partial.at[(far + f) * CORES + core_to, i],
            dst_ref=dst_ref,
            send_sem=part_send.at[3 + f * CORES + core_to, i],
            recv_sem=recv_sem,
            device_id=target,
            device_id_type=MESH,
        )

    far_blocks = [(f, core_to) for f in range(LINE // 2) for core_to in range(CORES)]

    def send_grads(i):
        own_copy(i).start()
        for step in range(1, plane):
            grad_copy(step, i).start()

    blocks = acts.shape[0]
    for way in range(2):
        @pl.when(line_next(0, way))
        def _():
            line_copy(0, way).start()

    for dx in range(1, chips):
        row_copy(z, dx, True).start()
    for block in range(blocks):
        act_own(block).start()
        act_copy(block).start()
    acc[...] = jnp.zeros_like(acc)

    def accumulate(block, features):
        act_own(block).wait()
        arrived(acts.at[block, 1], act_recv.at[block])
        tokens = acts.shape[2]
        both = acts[block].reshape(CORES * tokens, depth)
        acc[...] += jnp.dot(both, features, preferred_element_type=jnp.float32).reshape(acc.shape)

    def take_beside(k, way):
        for dx in range(1, chips):
            block = line_source(k, way) * chips + lax.rem(chip + dx, chips)
            arrived(proj_all.at[block], row_recv.at[block])
            if k < REACH:
                for onward in range(2) if k == 0 else (way,):
                    @pl.when(line_next(k, onward))
                    def _():
                        cross_copy(k, onward, dx).start()

            accumulate(block, proj_all[block])

    moments = [
        pltpu.make_async_copy(first_in, first_ref, moment_sem.at[0]),
        pltpu.make_async_copy(second_in, second_ref, moment_sem.at[1]),
    ]
    accumulate(z * chips + chip, proj_ref[...])
    for copy in moments:
        copy.start()
    take_beside(0, 0)
    send_grads(0)
    for k in range(1, LINE):
        for way in range(2):
            @pl.when(line_valid(k, way))
            def _():
                z_from = line_source(k, way)
                arrived(proj_all.at[z_from * chips + chip], line_recv.at[z_from])
                if k > REACH:
                    for dx in range(1, chips):
                        row_copy(z_from, dx).start()

            if k < LINE - 1:
                @pl.when(line_next(k, way))
                def _():
                    line_copy(k, way).start()

        for way in range(2):
            @pl.when(line_valid(k, way))
            def _():
                if k <= REACH:
                    take_beside(k, way)
                block = line_source(k, way) * chips + chip
                accumulate(block, proj_all[block])

        if k < LINE - 1:
            send_grads(k)
    for k in range(REACH + 1, LINE):
        for way in range(2):
            @pl.when(line_valid(k, way))
            def _():
                take_beside(k, way)

    acc_copy().start()
    arrived(acc_in, acc_recv)
    summed = jnp.transpose(acc[0] + acc_in[...]).astype(jnp.bfloat16)
    coords[...] = summed.reshape(coords.shape)
    each_coords_copy(lambda copy: copy.start())
    send_grads(LINE - 1)
    for q in range(parts):
        chip_to, own_block = coords_place(q)

        @pl.when(chip_to == chip)
        def _():
            coords_all[slot, own_block] = coords[q]

    for step in range(plane):
        source = in_plane(step)
        for block in range(LINE):
            if step:
                arrived(coords_all.at[source, block], coords_recv.at[source, block])
            else:
                @pl.when(lax.div(block * chips + chip, parts) != tp)
                def _():
                    arrived(coords_all.at[source, block], coords_recv.at[source, block])

    for i in range(LINE, AHEAD):
        send_grads(i)

    for copy in moments:
        copy.wait()

    def multiply(i):
        own_copy(i).wait()
        for step in range(1, plane):
            source = in_plane(step)
            arrived(grads.at[source, i], grad_recv.at[source, i])
        total = 0.0
        for source in range(plane):
            ranks = coords_all[source].reshape(LINE * CORES * rows, -1)
            total += jnp.dot(ranks, grads[source, i], preferred_element_type=jnp.float32)
        total = total.astype(jnp.bfloat16)
        for block in range(LINE * CORES):
            partial[block, i] = total[block * rows : (block + 1) * rows]
        @pl.when(jnp.logical_not(middle))
        def _():
            for f, core_to in far_blocks:
                far_copy(f, core_to, i, False).start()

        for index in range(1 + CORES):
            part_copy(index, i).start()
        landed[core, 0, i] = partial[z * CORES + core, i]

    def pass_on(i):
        @pl.when(middle)
        def _():
            for f, core_to in far_blocks:
                arrived(relay.at[f, core_to, i], relay_recv.at[f, core_to, i])
                block = (far + f) * CORES + core_to
                both = partial[block, i].astype(jnp.float32) + relay[f, core_to, i].astype(jnp.float32)
                partial[block, i] = both.astype(jnp.bfloat16)
                far_copy(f, core_to, i, True).start()

    def adam(i):
        for dc in range(CORES):
            core_from = lax.rem(core + dc, CORES)
            for place in range(0 if dc else 1, 3):
                arrived(landed.at[core_from, place, i], part_recv.at[core_from, place, i])
        for side in range(CORES):
            lowrank = landed[side, 0, i].astype(jnp.float32)
            for place in range(1, 3):
                lowrank += landed[side, place, i].astype(jnp.float32)
            columns = pl.ds(pl.multiple_of(side * half + i * width, 128), width)
            new_first = 0.9 * first_ref[:, columns] + 0.1 * lowrank
            new_second = 0.99 * second_ref[:, columns] + 0.01 * lowrank * lowrank
            lowrank_ref[:, columns] = lowrank
            direction_ref[:, columns] = (
                new_first / first_fix / (jnp.sqrt(new_second / second_fix) + 1e-08)
            ).astype(jnp.bfloat16)

    @pl.loop(0, CHUNKS)
    def _(i):
        @pl.when(i + AHEAD < CHUNKS)
        def _():
            send_grads(i + AHEAD)

        multiply(i)

        @pl.when(i >= 1)
        def _():
            pass_on(i - 1)

        @pl.when(i >= LAG)
        def _():
            adam(i - LAG)

    pass_on(CHUNKS - 1)

    @pl.loop(CHUNKS - LAG, CHUNKS)
    def _(i):
        adam(i)

    for k in range(LINE - 1):
        for way in range(2):
            @pl.when(line_next(k, way))
            def _():
                line_copy(k, way).wait_send()

    for dx in range(1, chips):
        row_copy(z, dx, True).wait_send()
    for k in range(REACH):
        for way in range(2):
            @pl.when(line_next(k, way))
            def _():
                for dx in range(1, chips):
                    cross_copy(k, way, dx).wait_send()

    for k in range(REACH + 1, LINE):
        for way in range(2):
            @pl.when(line_valid(k, way))
            def _():
                for dx in range(1, chips):
                    row_copy(line_source(k, way), dx).wait_send()

    for block in range(blocks):
        act_copy(block).wait_send()
    acc_copy().wait_send()
    each_coords_copy(lambda copy: copy.wait_send())

    @pl.loop(0, CHUNKS)
    def _(i):
        for step in range(1, plane):
            grad_copy(step, i).wait_send()
        for index in range(1 + CORES):
            part_copy(index, i).wait_send()
        for f, core_to in far_blocks:
            far_copy(f, core_to, i, True).wait_send()


def reduced(activations, proj_block, grad_output, first_moment, second_moment):
    tps = lax.axis_size("tp")
    plane = lax.axis_size("fsdp") // LINE
    blocks = plane * LINE // CORES
    tokens = activations.shape[0]
    depth, ranks = proj_block.shape
    rows, columns = first_moment.shape
    parts = ranks // (CORES * rows)
    width = columns // CORES // CHUNKS
    peers = LINE * CORES - 1
    dma = pltpu.SemaphoreType.DMA
    vmem = pl.BlockSpec(memory_space=pltpu.VMEM)
    hbm = pl.BlockSpec(memory_space=pl.ANY)
    return pl.pallas_call(
        reduce_kernel,
        out_shape=(
            jax.ShapeDtypeStruct((rows, columns), jnp.float32),
            jax.ShapeDtypeStruct((rows, columns), jnp.bfloat16),
        ),
        in_specs=[hbm, vmem, hbm, hbm, hbm],
        out_specs=(vmem, vmem),
        scratch_shapes=[
            pltpu.VMEM((blocks, depth, ranks), jnp.bfloat16),
            pltpu.VMEM((blocks, CORES, tokens, depth), jnp.bfloat16),
            pltpu.VMEM((CORES, tokens, ranks), jnp.float32),
            pltpu.VMEM((tokens, ranks), jnp.float32),
            pltpu.VMEM((parts, CORES * rows, tokens), jnp.bfloat16),
            pltpu.VMEM((plane, LINE, CORES * rows, tokens), jnp.bfloat16),
            pltpu.VMEM((plane, CHUNKS, tokens, width), jnp.bfloat16),
            pltpu.VMEM((LINE * CORES, CHUNKS, rows, width), jnp.bfloat16),
            pltpu.VMEM((CORES, 3, CHUNKS, rows, width), jnp.bfloat16),
            pltpu.VMEM((LINE // 2, CORES, CHUNKS, rows, width), jnp.bfloat16),
            pltpu.VMEM((rows, columns), jnp.float32),
            pltpu.VMEM((rows, columns), jnp.float32),
            dma((2,)),
            dma((2, LINE - 1)),
            dma((LINE,)),
            dma((2, REACH, plane // CORES)),
            dma((plane // CORES, LINE)),
            dma((blocks,)),
            dma((blocks,)),
            dma((blocks,)),
            dma((blocks,)),
            dma,
            dma,
            dma((parts, CORES * tps)),
            dma((plane, LINE)),
            dma((CHUNKS,)),
            dma((plane - 1, CHUNKS)),
            dma((plane, CHUNKS)),
            dma((peers, CHUNKS)),
            dma((CORES, 3, CHUNKS)),
            dma((LINE // 2, CORES, CHUNKS)),
        ],
        compiler_params=pltpu.CompilerParams(
            collective_id=0, has_side_effects=True, vmem_limit_bytes=62 * 2**20
        ),
        name="reduce_and_step",
    )(activations, proj_block, grad_output, first_moment, second_moment)


def update_kernel(projector_ref, direction_ref, out_ref):
    out_ref[...] = jnp.dot(
        projector_ref[...], direction_ref[...], preferred_element_type=jnp.float32
    ).astype(jnp.bfloat16)


def back_projected(projector, direction):
    rows, rank = projector.shape
    columns = direction.shape[1]
    width = columns // CHUNKS
    return pl.pallas_call(
        update_kernel,
        out_shape=jax.ShapeDtypeStruct((rows, columns), jnp.bfloat16),
        grid=(CHUNKS,),
        in_specs=[
            pl.BlockSpec((rows, rank), lambda i: (0, 0)),
            pl.BlockSpec((rank, width), lambda i: (0, i)),
        ],
        out_specs=pl.BlockSpec((rows, width), lambda i: (0, i)),
        compiler_params=pltpu.CompilerParams(vmem_limit_bytes=40 * 2**20),
        name="back_project",
    )(projector, direction)


def body(activations, grad_output, projector, first_moment, second_moment):
    rank_width = projector.shape[1]
    tp_count = lax.axis_size("tp")
    tp_place = lax.axis_index("tp")
    column_count = rank_width // tp_count
    proj_block = lax.dynamic_slice_in_dim(projector, tp_place * column_count, column_count, 1)
    lowrank, direction = reduced(
        activations, proj_block, grad_output, first_moment, second_moment
    )
    new_first = 0.9 * first_moment + 0.1 * lowrank
    new_second = 0.99 * second_moment + 0.01 * lowrank * lowrank
    direction_all = lax.all_gather(direction, "fsdp", axis=0, tiled=True)
    return (new_first, new_second, back_projected(projector, direction_all))


def solution(mesh):
    return jax.shard_map(
        body,
        mesh=mesh,
        in_specs=(
            P("fsdp", None),
            P("fsdp", "tp"),
            P("fsdp", None),
            P("fsdp", "tp"),
            P("fsdp", "tp"),
        ),
        out_specs=(P("fsdp", "tp"), P("fsdp", "tp"), P("fsdp", "tp")),
        check_vma=False,
    )
```
